512 devices in a mesh: outer: 4 (over x), grp: 16 (over z, core), span: 8 (over y).
Axes of the slice: x: 4, y: 8, z: 8, core: 2. Of those that a mesh axis runs over, the one named last changes fastest.
Arguments:
- embeddings: bfloat16 [131072, 1024], P(('outer', 'grp', 'span')), parts along dimension 0, may hold values from -6 to 6
- cluster_id: int32 [131072], P(('outer', 'grp', 'span')), parts along dimension 0, may hold values from 0 to 15, as said below
- member_order: int32 [131072], P(('outer', 'grp', 'span')), parts along dimension 0, may hold values from 0 to 32767, each once
Outputs:
- best_earlier: float32 [131072], P(('outer', 'grp', 'span')), parts along dimension 0
The draws below stay inside these ranges and needn't reach their ends.
There are 4 independent parts, one for each index of `outer`. The reference program is written for one: setup_inputs(seed, part) draws one part's arguments, and reference() takes and returns one part's arrays. A program takes and returns all parts, laid end to end along the dimension named above; each array names one. Nothing has to cross between parts.
Inputs may be any that keep to these rules, and one draw needn't show every extreme that they name: `cluster_id`: cluster c belongs to owner group c. The 256 embeddings of one device name clusters of one owner group at most 32 times; in every draw one owner group is named exactly 32 times by every device.
All inputs are finite; a program needn't handle non-finite values.
Results may differ from the reference program's by a relative error of at most 0.0003.
Values may be sent and summed in bfloat16 or wider, within the bound.
No kernel may reach another device: no remote copies, remote signals or barrier semaphores. Data moves between devices by JAX's collectives and lax.ppermute only.
A program may use at most 64 MiB of HBM per device.

```python
import jax
import jax.numpy as jnp
from jax import lax

D = 1024
ROWS_DEV = 256
CL_GRP = 1
CAPACITY = 32
TOTAL = 32768
N_GRP = 16
N_SPAN = 8


def draw_cluster_id(key, part):
    key = jax.random.fold_in(key, 11)
    device_total = N_GRP * N_SPAN
    slot_count = N_GRP * CAPACITY
    heavy_group = jax.random.randint(jax.random.fold_in(key, 1), (), 0, N_GRP)
    slot_group = jnp.repeat(jnp.arange(N_GRP, dtype=jnp.int32), CAPACITY)

    def per_device(device_index):
        device_key = jax.random.fold_in(key, device_index + 100)
        priority = jax.random.permutation(jax.random.fold_in(device_key, 1), slot_count).astype(jnp.int32)
        priority = jnp.where(slot_group == heavy_group, -1 - priority, priority)
        chosen = slot_group[jnp.argsort(priority, stable=True)[:ROWS_DEV]]
        shuffled = chosen[jax.random.permutation(jax.random.fold_in(device_key, 2), ROWS_DEV)]
        within = jax.random.randint(jax.random.fold_in(device_key, 3), (ROWS_DEV,), 0, CL_GRP)
        return shuffled * CL_GRP + within
    return jax.vmap(per_device)(jnp.arange(device_total)).reshape(-1).astype(jnp.int32)


def block_scale(key, shape, split, smallest, high):
    loudness, own = 1.0, jax.random.fold_in(key, 6)
    for position, parts in split:
        draws = jnp.exp(jax.random.uniform(jax.random.fold_in(own, position), (parts,), jnp.float32, smallest / len(split), high / len(split)))
        loudness = loudness * jnp.repeat(draws, shape[position] // parts).reshape([-1 if axis == position else 1 for axis in range(len(shape))])
    return loudness


def bell_draw(rng, dims, width, limit, split=(), kind=jnp.bfloat16):
    gain = block_scale(rng, dims, split, -0.22, 0.18) if split else 1.0
    values = jax.random.normal(rng, dims, jnp.float32) * width * gain
    return jnp.minimum(jnp.maximum(values, -limit), limit).astype(kind)


def setup_inputs(seed: int = 0, part: int = 0) -> dict:
    seeds = jax.random.split(jax.random.key(seed), 4)
    part_splits = jax.random.split(jax.random.fold_in(seeds[3], part), 4)
    return {
        "embeddings": bell_draw(part_splits[0], (TOTAL, D), 1.0, 6.0, ((0, 128),)),
        "cluster_id": draw_cluster_id(jax.random.fold_in(jax.random.fold_in(seeds[3], part), 71), part),
        "member_order": jax.random.permutation(part_splits[2], TOTAL).astype(jnp.int32),
    }


def inverse_norms(block_rows):
    widened = block_rows.astype(jnp.float32)
    return lax.rsqrt(lax.optimization_barrier(jnp.sum(widened * widened, axis=1)) + 1e-06)

def cosines(left_rows, left_norm, right_rows, right_norm):
    products = lax.dot_general(left_rows, right_rows, (((1,), (1,)), ((), ())), preferred_element_type=jnp.float32)
    return products * left_norm[:, None] * right_norm[None, :]

def reference(embeddings, cluster_id, member_order):
    all_norm = inverse_norms(embeddings)
    block_count = TOTAL // ROWS_DEV

    def one_block(inputs):
        block_rows, block_norm, block_cluster, block_order = inputs
        scores = cosines(block_rows, block_norm, embeddings, all_norm)
        earlier = (block_cluster[:, None] == cluster_id[None, :]) & (member_order[None, :] < block_order[:, None])
        return lax.optimization_barrier(jnp.max(jnp.where(earlier, scores, jnp.float32(-1.0)), axis=1))
    result = lax.map(one_block, (embeddings.reshape(block_count, ROWS_DEV, D), all_norm.reshape(block_count, ROWS_DEV), cluster_id.reshape(block_count, ROWS_DEV), member_order.reshape(block_count, ROWS_DEV)))
    return result.reshape(TOTAL)
```

```python
import functools

import jax
import jax.numpy as jnp
from jax import lax
from jax.experimental import pallas as pl
from jax.experimental.pallas import tpu as pltpu
from jax.sharding import PartitionSpec as P

ROWS = 256
META = 16
AUG = ROWS + META
SPAN_ORDER = 32768
LOW = -1e30
VMEM_LIMIT = 48 * 1024 * 1024


def prepare_kernel(x_ref, cluster_ref, order_ref, aug_ref, norm_ref):
    rows = x_ref[...]
    wide = rows.astype(jnp.float32)
    column = lax.rsqrt(jnp.sum(wide * wide, axis=1, keepdims=True) + 1e-06)
    norm = jnp.broadcast_to(column, (ROWS, 128)).T[0:1, :]
    cluster = cluster_ref[...].astype(jnp.float32)
    order = order_ref[...]
    high = jnp.right_shift(order, 8).astype(jnp.float32)
    low = jnp.bitwise_and(order, 255).astype(jnp.float32)
    first = norm.astype(jnp.bfloat16).astype(jnp.float32)
    rest = norm - first
    second = rest.astype(jnp.bfloat16).astype(jnp.float32)
    third = rest - second
    line = lax.broadcasted_iota(jnp.int32, (META, ROWS), 0)
    meta = jnp.zeros((META, ROWS), jnp.float32)
    for index, values in enumerate((cluster, high, low, first, second, third)):
        meta = jnp.where(line == index, values, meta)
    aug_ref[0:ROWS, :] = rows
    aug_ref[ROWS:AUG, :] = jnp.zeros((META, rows.shape[1]), jnp.bfloat16)
    aug_ref[ROWS:AUG, 0:ROWS] = meta.astype(jnp.bfloat16)
    norm_ref[...] = norm


def prepare(x, cluster, order):
    return pl.pallas_call(
        prepare_kernel,
        out_shape=(
            jax.ShapeDtypeStruct((AUG, x.shape[1]), jnp.bfloat16),
            jax.ShapeDtypeStruct((1, ROWS), jnp.float32),
        ),
        compiler_params=pltpu.CompilerParams(vmem_limit_bytes=VMEM_LIMIT),
    )(x, cluster.reshape(1, ROWS), order.reshape(1, ROWS))


def read_meta(ref):
    meta = ref[ROWS:AUG, 0:ROWS].astype(jnp.float32)
    floor = meta[0:1] * float(SPAN_ORDER)
    key = floor + (meta[1:2] * 256.0 + meta[2:3])
    norm = meta[3:4] + (meta[4:5] + meta[5:6])
    return floor, key, norm


def fold_kernel(n_old_rows, n_new_rows, n_old_cols, n_new_cols, has_acc, *refs):
    refs = list(refs)
    take = lambda n: [refs.pop(0) for _ in range(n)]
    rows = take(n_old_rows + n_new_rows)
    cols = take(n_old_cols + n_new_cols)
    old_wide = take(n_old_cols)
    acc_in = take(1) if has_acc else []
    acc_ref = refs.pop(0)
    new_wide = take(n_new_cols)
    row_data, row_key, row_floor = refs
    n_rows = n_old_rows + n_new_rows

    for i, ref in enumerate(rows):
        row_data[i] = ref[0:ROWS, :]
        floor, key, _ = read_meta(ref)
        row_key[i] = jnp.broadcast_to(key, (8, ROWS))
        row_floor[i] = jnp.broadcast_to(floor, (8, ROWS))
    for ref, wide in zip(cols[n_old_cols:], new_wide):
        _, key, norm = read_meta(ref)
        for half in range(2):
            part = slice(half * 128, (half + 1) * 128)
            wide[part, 0:128] = jnp.broadcast_to(key[:, part], (128, 128)).T
            wide[part, 128:256] = jnp.broadcast_to(norm[:, part], (128, 128)).T
    wides = old_wide + new_wide

    def block(i, picked, best):
        right = row_data[i]
        for j in picked:
            score = lax.dot_general(
                cols[j][0:ROWS, :], right, (((1,), (1,)), ((), ())), preferred_element_type=jnp.float32
            )
            halves = []
            for half in range(2):
                part = slice(half * 128, (half + 1) * 128)
                key = wides[j][:, 0:128].reshape(ROWS // 8, 8, 128)
                norm = wides[j][:, 128:256].reshape(ROWS // 8, 8, 128)
                valid = (key < row_key[i, :, part]) & (key >= row_floor[i, :, part])
                scaled = score[:, part].reshape(ROWS // 8, 8, 128) * norm
                halves.append(jnp.max(jnp.where(valid, scaled, LOW), axis=0))
            best = jnp.maximum(best, jnp.concatenate(halves, axis=1))
        return best

    def old_row(i, carry):
        acc_ref[i] = block(i, range(n_old_cols, n_old_cols + n_new_cols), acc_in[0][i])
        return carry

    def new_row(i, carry):
        start = jnp.full((8, ROWS), LOW, jnp.float32)
        acc_ref[i] = block(i, range(n_old_cols + n_new_cols), start)
        return carry

    if n_old_rows and n_new_cols:
        lax.fori_loop(0, n_old_rows, old_row, 0)
    elif n_old_rows:
        acc_ref[0:n_old_rows] = acc_in[0][...]
    if n_new_rows:
        lax.fori_loop(n_old_rows, n_rows, new_row, 0)


def fold(old_rows, new_rows, old_cols, new_cols, old_wide, acc):
    n_rows = len(old_rows) + len(new_rows)
    has_acc = acc is not None
    width = (old_rows + new_rows)[0].shape[1]
    pairs = len(new_rows) * (len(old_cols) + len(new_cols)) + len(old_rows) * len(new_cols)
    args = [*old_rows, *new_rows, *old_cols, *new_cols, *old_wide, *([acc] if has_acc else [])]
    out = pl.pallas_call(
        functools.partial(
            fold_kernel, len(old_rows), len(new_rows), len(old_cols), len(new_cols), has_acc
        ),
        out_shape=(
            jax.ShapeDtypeStruct((n_rows, 8, ROWS), jnp.float32),
            *[jax.ShapeDtypeStruct((ROWS, 256), jnp.float32) for _ in new_cols],
        ),
        scratch_shapes=[
            pltpu.VMEM((n_rows, ROWS, width), jnp.bfloat16),
            pltpu.VMEM((n_rows, 8, ROWS), jnp.float32),
            pltpu.VMEM((n_rows, 8, ROWS), jnp.float32),
        ],
        compiler_params=pltpu.CompilerParams(vmem_limit_bytes=VMEM_LIMIT),
        cost_estimate=pl.CostEstimate(
            flops=2 * pairs * ROWS * ROWS * width, bytes_accessed=len(args) * AUG * width * 2, transcendentals=0
        ),
    )(*args)
    return out[0], list(out[1:])


def route_kernel(offsets, place_ref, acc_ref, out_ref):
    here = place_ref[0]
    for index, offset in enumerate(offsets):
        target = lax.rem(here + offset, 8)
        out_ref[pl.ds(target, 1), :] = jnp.max(acc_ref[index], axis=0, keepdims=True)


def route(acc, place, offsets):
    return pl.pallas_call(
        functools.partial(route_kernel, offsets),
        out_shape=jax.ShapeDtypeStruct((8, ROWS), jnp.float32),
        in_specs=[pl.BlockSpec(memory_space=pltpu.SMEM), pl.BlockSpec(memory_space=pltpu.VMEM)],
        out_specs=pl.BlockSpec(memory_space=pltpu.VMEM),
    )(place, acc)


def ring(axis, size, step):
    return [(i, (i + step) % size) for i in range(size)]


def per_device(embeddings, cluster_id, member_order):
    own, norm = prepare(embeddings, cluster_id, member_order)
    swap = lambda v: lax.ppermute(v, "grp", [(i, i ^ 1) for i in range(16)])
    y_up = lambda v: lax.ppermute(v, "span", ring("span", 8, 1))
    y_down = lambda v: lax.ppermute(v, "span", ring("span", 8, -1))
    z_up = lambda v: lax.ppermute(v, "grp", ring("grp", 16, 2))
    z_down = lambda v: lax.ppermute(v, "grp", ring("grp", 16, -2))

    ya, yb, za, zb = [own], [own], [own], [own]
    for _ in range(3):
        ya.append(y_up(ya[-1]))
        yb.append(y_down(yb[-1]))
        za.append(z_up(za[-1]))
        zb.append(z_down(zb[-1]))
    ya.append(y_up(ya[-1]))
    zb.append(z_down(zb[-1]))

    sibling = swap(own)

    def swapped(blocks):
        joined = swap(jnp.concatenate(blocks, axis=0))
        return [joined[AUG * i : AUG * (i + 1)] for i in range(len(blocks))]

    near = swapped([ya[1], yb[1], ya[2], yb[2]])
    far = swapped([ya[3], yb[3], ya[4]])

    rows, cols, wides, acc = [], [], [], None
    steps = [
        ([own, za[1], zb[1]], [own, sibling, ya[1], yb[1]]),
        ([za[2], zb[2]], [ya[2], yb[2]]),
        ([], near),
        ([za[3], zb[3]], [ya[3], yb[3]]),
        ([zb[4]], [ya[4]]),
        ([], far),
    ]
    for new_rows, new_cols in steps:
        acc, more = fold(rows, new_rows, cols, new_cols, wides if new_rows else [], acc) if new_rows else fold(
            rows, [], [], new_cols, [], acc
        )
        rows, cols, wides = rows + new_rows, cols + new_cols, wides + more

    offsets = (0, 7, 1, 6, 2, 5, 3, 4)
    place = (lax.axis_index("grp") // 2).astype(jnp.int32).reshape(1)
    outgoing = route(acc, place, offsets)
    groups = [[2 * z + core for z in range(8)] for core in range(2)]
    arrived = lax.all_to_all(
        outgoing, "grp", split_axis=0, concat_axis=0, tiled=True, axis_index_groups=groups
    )
    return jnp.maximum(jnp.max(arrived, axis=0) * norm[0], -1.0)


def solution(mesh):
    return jax.shard_map(
        per_device,
        mesh=mesh,
        in_specs=(
            P(("outer", "grp", "span"), None),
            P(("outer", "grp", "span")),
            P(("outer", "grp", "span")),
        ),
        out_specs=P(("outer", "grp", "span")),
        check_vma=False,
    )
```

```python
import functools

import jax
import jax.numpy as jnp
from jax import lax
from jax.experimental import pallas as pl
from jax.experimental.pallas import tpu as pltpu
from jax.sharding import PartitionSpec as P

ROWS = 256
CLUSTERS = 16
SLOTS = 32
WINDOW = 48
ORDERS = 32768.0
LOW = -1e30
MIB = 1024 * 1024
META = 16
AUG = ROWS + META
START = 7


def iota(shape, dimension):
    return lax.broadcasted_iota(jnp.int32, shape, dimension)


def turn(line):
    return jnp.concatenate([jnp.broadcast_to(line[:, h : h + 128], (128, 128)).T for h in (0, 128)], axis=0)


def tall(meta):
    filled = jnp.concatenate([meta, jnp.zeros((128 - META, ROWS), meta.dtype)], axis=0)
    return jnp.concatenate([filled[:, 0:128].T, filled[:, 128:256].T], axis=0)


def prepare_kernel(x_ref, cluster_ref, order_ref, aug_ref, norm_ref, slot_ref):
    rows = x_ref[...]
    wide = rows.astype(jnp.float32)
    norm = jnp.broadcast_to(lax.rsqrt(jnp.sum(wide * wide, axis=1, keepdims=True) + 1e-06), (ROWS, 128))
    norm = jnp.concatenate([norm[0:128, :].T[0:1, :], norm[128:256, :].T[0:1, :]], axis=1)
    cluster = cluster_ref[...].astype(jnp.float32)
    order = order_ref[...]
    floor = cluster * ORDERS
    key = floor + order.astype(jnp.float32)
    key_down = jnp.concatenate([turn(key)] * 2, axis=1)
    rank = jnp.sum((key_down < key).astype(jnp.float32), axis=0, keepdims=True)
    inside = rank - jnp.sum((key_down < floor).astype(jnp.float32), axis=0, keepdims=True)
    high = jnp.right_shift(order, 8).astype(jnp.float32)
    low = jnp.bitwise_and(order, 255).astype(jnp.float32)
    first = norm.astype(jnp.bfloat16).astype(jnp.float32)
    second = (norm - first).astype(jnp.bfloat16).astype(jnp.float32)
    third = norm - first - second

    line, lane = iota((META, ROWS), 0), iota((META, ROWS), 1)
    meta = jnp.zeros((META, ROWS), jnp.float32)
    for index, values in enumerate((cluster, high, low, first, second, third, inside)):
        meta = jnp.where(line == index, values, meta)
    permute = (iota((ROWS, ROWS), 0).astype(jnp.float32) == rank).astype(jnp.bfloat16)
    meta = by_lines(meta.astype(jnp.bfloat16), permute)
    count = jnp.sum((turn(cluster) < iota((ROWS, 128), 1).astype(jnp.float32)).astype(jnp.float32), axis=0, keepdims=True)
    start = jnp.minimum(jnp.bitwise_and(count.astype(jnp.int32), -16), ROWS - WINDOW).astype(jnp.float32)
    meta = jnp.where(line == START, jnp.concatenate([start] * 2, axis=1), meta)

    aug_ref[0:ROWS, :] = jnp.dot(permute, rows, preferred_element_type=jnp.float32).astype(jnp.bfloat16)
    aug_ref[ROWS:AUG, :] = jnp.zeros((META, rows.shape[1]), jnp.bfloat16)
    aug_ref[ROWS:AUG, 0:ROWS] = meta.astype(jnp.bfloat16)
    norm_ref[...] = norm
    slot_ref[...] = cluster * float(SLOTS) + inside


def prepare(x, cluster, order):
    return pl.pallas_call(
        prepare_kernel,
        out_shape=(
            jax.ShapeDtypeStruct((AUG, x.shape[1]), jnp.bfloat16),
            jax.ShapeDtypeStruct((1, ROWS), jnp.float32),
            jax.ShapeDtypeStruct((1, ROWS), jnp.float32),
        ),
        compiler_params=pltpu.CompilerParams(vmem_limit_bytes=16 * MIB),
    )(x, cluster.reshape(1, ROWS), order.reshape(1, ROWS))


def line_weights():
    line, lane = iota((16, 128), 0), iota((16, 128), 1)
    weights = jnp.zeros((16, 128), jnp.float32)
    for at, of, weight in ((0, 0, ORDERS), (0, 1, 256.0), (0, 2, 1.0), (1, 0, ORDERS)):
        weights = jnp.where((line == at) & (lane == of), weight, weights)
    return weights.astype(jnp.bfloat16)


def spread_weights():
    line, lane = iota((128, 256), 0), iota((128, 256), 1)
    weights = jnp.zeros((128, 256), jnp.float32)
    for of, weight in ((0, ORDERS), (1, 256.0), (2, 1.0)):
        weights = jnp.where((line == of) & (lane < 128), weight, weights)
    return jnp.where((line >= 3) & (line <= 5) & (lane >= 128), 1.0, weights).astype(jnp.bfloat16)


def by_lines(weights, meta):
    return lax.dot_general(weights, meta, (((1,), (1,)), ((), ())), preferred_element_type=jnp.float32)


def match_kernel(offsets, table_ref, place_ref, *refs):
    rows = refs[: len(offsets)]
    cols_ref, out_ref, held, held_meta, slots, slot_meta, sem = refs[len(offsets) :]
    blocks = cols_ref.shape[0] // AUG
    width = held.shape[2]
    copies = [
        pltpu.make_async_copy(cols_ref.at[b * AUG : (b + 1) * AUG, :], held.at[b], sem.at[b]) for b in range(blocks)
    ]
    for copy in copies:
        copy.start()
    for ref, offset in zip(rows, offsets):
        meta = ref[ROWS:AUG, 0:ROWS]
        wide = meta.astype(jnp.float32)
        slot = wide[0:1] * float(SLOTS) + wide[6:7]
        pick = (iota((CLUSTERS * SLOTS, ROWS), 0).astype(jnp.float32) == slot).astype(jnp.bfloat16)
        home = pl.multiple_of(lax.rem(place_ref[0] + offset, 8) * SLOTS, SLOTS)
        spread = jnp.dot(pick, ref[0:ROWS, :], preferred_element_type=jnp.float32).astype(jnp.bfloat16)
        slots[:, pl.ds(home, SLOTS), :] = spread.reshape(CLUSTERS, SLOTS, width)
        spread = jnp.dot(pick, tall(meta), preferred_element_type=jnp.float32).astype(jnp.bfloat16)
        slot_meta[:, pl.ds(home, SLOTS), :] = spread.reshape(CLUSTERS, SLOTS, 128)
    for b, copy in enumerate(copies):
        copy.wait()
        held_meta[b] = tall(held[b, ROWS:AUG, 0:ROWS])
    groups = blocks * WINDOW // 8

    def cluster(g, carry):
        starts = [pl.multiple_of(table_ref[b, g], 16) for b in range(blocks)]
        window = jnp.concatenate([held[b, pl.ds(starts[b], WINDOW), :] for b in range(blocks)], axis=0)
        window_meta = jnp.concatenate([held_meta[b, pl.ds(starts[b], WINDOW), :] for b in range(blocks)], axis=0)
        score = lax.dot_general(
            window, slots[g], (((1,), (1,)), ((), ())), preferred_element_type=jnp.float32
        )
        col = jnp.dot(window_meta, spread_weights(), preferred_element_type=jnp.float32)
        row = by_lines(line_weights(), slot_meta[g])
        key = col[:, 0:128].reshape(groups, 8, 128)
        norm = col[:, 128:256].reshape(groups, 8, 128)
        halves = []
        for half in (0, 128):
            row_key, row_floor = row[0:1, half : half + 128], row[1:2, half : half + 128]
            valid = (key < row_key) & (key >= row_floor)
            scaled = score[:, half : half + 128].reshape(groups, 8, 128) * norm
            halves.append(jnp.max(jnp.where(valid, scaled, LOW), axis=0))
        best = jnp.concatenate(halves, axis=1)
        out_ref[g] = jnp.max(best, axis=0, keepdims=True)
        return carry

    lax.fori_loop(0, CLUSTERS, cluster, 0, unroll=UNROLL)


UNROLL = 2


def match(table, place, rows, offsets, cols):
    width = cols.shape[1]
    blocks = cols.shape[0] // AUG
    vmem, smem = pl.BlockSpec(memory_space=pltpu.VMEM), pl.BlockSpec(memory_space=pltpu.SMEM)
    return pl.pallas_call(
        functools.partial(match_kernel, offsets),
        out_shape=jax.ShapeDtypeStruct((CLUSTERS, 1, 8 * SLOTS), jnp.float32),
        in_specs=[smem, smem] + [vmem] * len(rows) + [pl.BlockSpec(memory_space=pltpu.HBM)],
        out_specs=vmem,
        scratch_shapes=[
            pltpu.VMEM((blocks, AUG, width), jnp.bfloat16),
            pltpu.VMEM((blocks, ROWS, 128), jnp.bfloat16),
            pltpu.VMEM((CLUSTERS, 8 * SLOTS, width), jnp.bfloat16),
            pltpu.VMEM((CLUSTERS, 8 * SLOTS, 128), jnp.bfloat16),
            pltpu.SemaphoreType.DMA((blocks,)),
        ],
        compiler_params=pltpu.CompilerParams(vmem_limit_bytes=44 * MIB),
    )(table, place, *rows, cols)


def collect_kernel(found_ref, slot_ref, norm_ref, out_ref):
    found = jnp.max(found_ref[...], axis=0, keepdims=True)
    column = jnp.concatenate([turn(found[:, h : h + 256]) for h in (0, 256)], axis=0)
    for half in (0, 128):
        slot = slot_ref[:, half : half + 128]
        mine = iota((CLUSTERS * SLOTS, 128), 0).astype(jnp.float32) == slot
        best = jnp.max(jnp.where(mine, column, LOW), axis=0, keepdims=True)
        out_ref[:, half : half + 128] = jnp.maximum(best * norm_ref[:, half : half + 128], -1.0)


def collect(found, slot, norm):
    return pl.pallas_call(
        collect_kernel,
        out_shape=jax.ShapeDtypeStruct((1, ROWS), jnp.float32),
    )(found, slot, norm)


def ring(size, step):
    return [(i, (i + step) % size) for i in range(size)]


def per_device(embeddings, cluster_id, member_order):
    own, norm, slot = prepare(embeddings, cluster_id, member_order)
    cols = lax.all_gather(own, "grp", axis=0, tiled=True)
    tables = cols.reshape(16, AUG, embeddings.shape[1])[:, ROWS + START, 0:CLUSTERS].astype(jnp.int32)

    up = lambda v: lax.ppermute(v, "span", ring(8, 1))
    down = lambda v: lax.ppermute(v, "span", ring(8, -1))
    blocks, u, d = [own], own, own
    for _ in range(3):
        u, d = up(u), down(d)
        blocks += [u, d]
    blocks.append(up(u))
    place = lax.axis_index("span").astype(jnp.int32).reshape(1)
    found = match(tables, place, blocks, (0, 7, 1, 6, 2, 5, 3, 4), cols).reshape(CLUSTERS, 8, SLOTS)
    found = found.transpose(1, 0, 2).reshape(8, CLUSTERS * SLOTS)
    arrived = lax.all_to_all(found, "span", split_axis=0, concat_axis=0, tiled=True)
    return collect(arrived, slot, norm)[0]


def solution(mesh):
    return jax.shard_map(
        per_device,
        mesh=mesh,
        in_specs=(
            P(("outer", "grp", "span"), None),
            P(("outer", "grp", "span")),
            P(("outer", "grp", "span")),
        ),
        out_specs=P(("outer", "grp", "span")),
        check_vma=False,
    )
```

```python
import functools

import jax
import jax.numpy as jnp
from jax import lax
from jax.experimental import pallas as pl
from jax.experimental.pallas import tpu as pltpu
from jax.sharding import PartitionSpec as P

ROWS = 256
CLUSTERS = 16
SLOTS = 32
WINDOW = 48
ORDERS = 32768.0
LOW = -1e30
MIB = 1024 * 1024
META = 16
AUG = ROWS + META
START = 7


def iota(shape, dimension):
    return lax.broadcasted_iota(jnp.int32, shape, dimension)


def turn(line):
    return jnp.concatenate([jnp.broadcast_to(line[:, h : h + 128], (128, 128)).T for h in (0, 128)], axis=0)


def tall(meta):
    filled = jnp.concatenate([meta, jnp.zeros((128 - META, ROWS), meta.dtype)], axis=0)
    return jnp.concatenate([filled[:, 0:128].T, filled[:, 128:256].T], axis=0)


def row_facts(rows, cluster, order):
    wide = rows.astype(jnp.float32)
    norm = jnp.broadcast_to(lax.rsqrt(jnp.sum(wide * wide, axis=1, keepdims=True) + 1e-06), (ROWS, 128))
    norm = jnp.concatenate([norm[0:128, :].T[0:1, :], norm[128:256, :].T[0:1, :]], axis=1)
    floor = cluster * ORDERS
    key = floor + order
    key_down = jnp.concatenate([turn(key)] * 2, axis=1)
    rank = jnp.sum((key_down < key).astype(jnp.float32), axis=0, keepdims=True)
    inside = rank - jnp.sum((key_down < floor).astype(jnp.float32), axis=0, keepdims=True)
    return norm, rank, inside


def staged(refs, held, sem):
    copies = [pltpu.make_async_copy(ref, to, sem.at[i]) for i, (ref, to) in enumerate(zip(refs, held))]
    for copy in copies:
        copy.start()
    for copy in copies:
        copy.wait()


def prepare_kernel(x_hbm, cluster_hbm, order_hbm, aug_ref, x_ref, cluster_ref, order_ref, sem):
    staged((x_hbm, cluster_hbm, order_hbm), (x_ref, cluster_ref, order_ref), sem)
    rows = x_ref[...]
    cluster = cluster_ref[...].astype(jnp.float32)
    order = order_ref[...]
    norm, rank, inside = row_facts(rows, cluster, order.astype(jnp.float32))
    high = jnp.right_shift(order, 8).astype(jnp.float32)
    low = jnp.bitwise_and(order, 255).astype(jnp.float32)
    first = norm.astype(jnp.bfloat16).astype(jnp.float32)
    second = (norm - first).astype(jnp.bfloat16).astype(jnp.float32)
    third = norm - first - second

    line = iota((META, ROWS), 0)
    meta = jnp.zeros((META, ROWS), jnp.float32)
    for index, values in enumerate((cluster, high, low, first, second, third, inside)):
        meta = jnp.where(line == index, values, meta)
    permute = (iota((ROWS, ROWS), 0).astype(jnp.float32) == rank).astype(jnp.bfloat16)
    meta = by_lines(meta.astype(jnp.bfloat16), permute)
    count = jnp.sum((turn(cluster) < iota((ROWS, 128), 1).astype(jnp.float32)).astype(jnp.float32), axis=0, keepdims=True)
    start = jnp.minimum(jnp.bitwise_and(count.astype(jnp.int32), -16), ROWS - WINDOW).astype(jnp.float32)
    meta = jnp.where(line == START, jnp.concatenate([start] * 2, axis=1), meta)

    aug_ref[0:ROWS, :] = jnp.dot(permute, rows, preferred_element_type=jnp.float32).astype(jnp.bfloat16)
    aug_ref[ROWS:AUG, :] = jnp.zeros((META, rows.shape[1]), jnp.bfloat16)
    aug_ref[ROWS:AUG, 0:ROWS] = meta.astype(jnp.bfloat16)


def remember_kernel(x_hbm, cluster_hbm, order_hbm, out_ref, x_ref, cluster_ref, order_ref, sem):
    staged((x_hbm, cluster_hbm, order_hbm), (x_ref, cluster_ref, order_ref), sem)
    cluster = cluster_ref[...].astype(jnp.float32)
    norm, _, inside = row_facts(x_ref[...], cluster, order_ref[...].astype(jnp.float32))
    out_ref[0:1, :] = norm
    out_ref[1:2, :] = cluster * float(SLOTS) + inside


def own_call(kernel, out, x, cluster, order):
    return pl.pallas_call(
        kernel,
        out_shape=out,
        in_specs=[pl.BlockSpec(memory_space=pltpu.HBM)] * 3,
        scratch_shapes=[
            pltpu.VMEM(x.shape, x.dtype),
            pltpu.VMEM((1, ROWS), jnp.int32),
            pltpu.VMEM((1, ROWS), jnp.int32),
            pltpu.SemaphoreType.DMA((3,)),
        ],
        compiler_params=pltpu.CompilerParams(vmem_limit_bytes=OWN_LIMIT * MIB),
    )(x, cluster.reshape(1, ROWS), order.reshape(1, ROWS))


def line_weights():
    line, lane = iota((16, 128), 0), iota((16, 128), 1)
    weights = jnp.zeros((16, 128), jnp.float32)
    for at, of, weight in ((0, 0, ORDERS), (0, 1, 256.0), (0, 2, 1.0), (1, 0, ORDERS)):
        weights = jnp.where((line == at) & (lane == of), weight, weights)
    return weights.astype(jnp.bfloat16)


def spread_weights():
    line, lane = iota((128, 256), 0), iota((128, 256), 1)
    weights = jnp.zeros((128, 256), jnp.float32)
    for of, weight in ((0, ORDERS), (1, 256.0), (2, 1.0)):
        weights = jnp.where((line == of) & (lane < 128), weight, weights)
    return jnp.where((line >= 3) & (line <= 5) & (lane >= 128), 1.0, weights).astype(jnp.bfloat16)


def by_lines(weights, meta):
    return lax.dot_general(weights, meta, (((1,), (1,)), ((), ())), preferred_element_type=jnp.float32)


def into_slots(rows, meta):
    wide = meta.astype(jnp.float32)
    slot = wide[0:1] * float(SLOTS) + wide[6:7]
    pick = (iota((CLUSTERS * SLOTS, ROWS), 0).astype(jnp.float32) == slot).astype(jnp.bfloat16)
    both = [jnp.dot(pick, v, preferred_element_type=jnp.float32).astype(jnp.bfloat16) for v in (rows, tall(meta))]
    return [v.reshape(CLUSTERS, SLOTS, v.shape[1]) for v in both]


def home(place_ref, offset):
    return pl.ds(pl.multiple_of(lax.rem(place_ref[0] + offset, 8) * SLOTS, SLOTS), SLOTS)


def spread_kernel(offsets, place_ref, *refs):
    slots, slot_meta = refs[-2:]
    for ref, offset in zip(refs, offsets):
        at = home(place_ref, offset)
        slots[:, at, :], slot_meta[:, at, :] = into_slots(ref[0:ROWS, :], ref[ROWS:AUG, 0:ROWS])


def spread(place, rows, offsets):
    vmem, smem = pl.BlockSpec(memory_space=pltpu.VMEM), pl.BlockSpec(memory_space=pltpu.SMEM)
    width = rows[0].shape[1]
    return pl.pallas_call(
        functools.partial(spread_kernel, offsets),
        out_shape=(
            jax.ShapeDtypeStruct((CLUSTERS, 8 * SLOTS, width), jnp.bfloat16),
            jax.ShapeDtypeStruct((CLUSTERS, 8 * SLOTS, 128), jnp.bfloat16),
        ),
        in_specs=[smem] + [vmem] * len(rows),
        out_specs=(vmem, vmem),
        compiler_params=pltpu.CompilerParams(vmem_limit_bytes=24 * MIB),
    )(place, *rows)


OWN_LIMIT = 56
MATCH_LIMIT = 52
TOP = 144
TEAM = 4


def match_kernel(
    offset, table_ref, place_ref, last_ref, slots_hbm, slot_meta_hbm, cols_hbm, out_ref,
    held, held_lanes, slots, slot_meta, slot_lines, last_slots, last_meta, waited, sem,
):
    blocks = cols_hbm.shape[0] // AUG

    def part(b, first, last, kind):
        source = cols_hbm.at[b * AUG + first : b * AUG + last, :]
        return pltpu.make_async_copy(source, held.at[b, first:last, :], sem.at[kind, b])

    def team(k):
        at = pl.ds(k * TEAM, TEAM)
        return pltpu.make_async_copy(slots_hbm.at[at], slots.at[at], sem.at[3, k])

    notes = [part(b, ROWS, AUG, 0) for b in range(blocks)]
    tops = [part(b, 0, TOP, 1) for b in range(blocks)]
    rests = [part(b, TOP, ROWS, 2) for b in range(blocks)]
    small = pltpu.make_async_copy(slot_meta_hbm, slot_meta, sem.at[4, 0])
    for copy in [*notes, small, *tops, team(0), *rests] + [team(k) for k in range(1, CLUSTERS // TEAM)]:
        copy.start()
    waited[0] = 0
    last_slots[...], last_meta[...] = into_slots(last_ref[0:ROWS, :], last_ref[ROWS:AUG, 0:ROWS])
    weights = spread_weights()
    for b, copy in enumerate(notes):
        copy.wait()
        meta = tall(held[b, ROWS:AUG, 0:ROWS])
        held_lanes[b] = jnp.dot(meta, weights, preferred_element_type=jnp.float32)
    at = home(place_ref, offset)
    small.wait()
    slot_meta[:, at, :] = last_meta[...]
    weights = line_weights()
    for g in range(CLUSTERS):
        slot_lines[g] = by_lines(weights, slot_meta[g])[0:8]
    for copy in tops:
        copy.wait()
    groups = blocks * WINDOW // 8

    def cluster(g):
        starts = [pl.multiple_of(table_ref[b, g], 16) for b in range(blocks)]
        window = jnp.concatenate([held[b, pl.ds(starts[b], WINDOW), :] for b in range(blocks)], axis=0)
        lanes = jnp.concatenate([held_lanes[b, pl.ds(starts[b], WINDOW), :] for b in range(blocks)], axis=0)
        score = by_lines(window, slots[g])
        key = lanes[:, 0:128].reshape(groups, 8, 128)
        norm = lanes[:, 128:256].reshape(groups, 8, 128)
        halves = []
        for half in (0, 128):
            row_key, row_floor = slot_lines[g, 0:1, half : half + 128], slot_lines[g, 1:2, half : half + 128]
            valid = (key < row_key) & (key >= row_floor)
            scaled = score[:, half : half + 128].reshape(groups, 8, 128) * norm
            halves.append(jnp.max(jnp.where(valid, scaled, LOW), axis=0))
        best = jnp.concatenate(halves, axis=1)
        out_ref[g] = jnp.max(best, axis=0, keepdims=True)

    def step(k, carry):
        end = functools.reduce(jnp.maximum, [table_ref[b, k * TEAM + TEAM - 1] for b in range(blocks)]) + WINDOW

        @pl.when((waited[0] == 0) & ((end > TOP) | (k == CLUSTERS // TEAM - 1)))
        def _():
            for copy in rests:
                copy.wait()
            waited[0] = 1

        team(k).wait()
        of = pl.ds(k * TEAM, TEAM)
        slots[of, at, :] = last_slots[of]
        for i in range(TEAM):
            cluster(k * TEAM + i)
        return carry

    lax.fori_loop(0, CLUSTERS // TEAM, step, 0)


def match(table, place, last, offset, slots, slot_meta, cols):
    width = cols.shape[1]
    blocks = cols.shape[0] // AUG
    vmem, smem = pl.BlockSpec(memory_space=pltpu.VMEM), pl.BlockSpec(memory_space=pltpu.SMEM)
    hbm = pl.BlockSpec(memory_space=pltpu.HBM)
    return pl.pallas_call(
        functools.partial(match_kernel, offset),
        out_shape=jax.ShapeDtypeStruct((CLUSTERS, 1, 8 * SLOTS), jnp.float32),
        in_specs=[smem, smem, vmem, hbm, hbm, hbm],
        out_specs=vmem,
        scratch_shapes=[
            pltpu.VMEM((blocks, AUG, width), jnp.bfloat16),
            pltpu.VMEM((blocks, ROWS, 256), jnp.float32),
            pltpu.VMEM((CLUSTERS, 8 * SLOTS, width), jnp.bfloat16),
            pltpu.VMEM((CLUSTERS, 8 * SLOTS, 128), jnp.bfloat16),
            pltpu.VMEM((CLUSTERS, 8, 8 * SLOTS), jnp.float32),
            pltpu.VMEM((CLUSTERS, SLOTS, width), jnp.bfloat16),
            pltpu.VMEM((CLUSTERS, SLOTS, 128), jnp.bfloat16),
            pltpu.SMEM((1,), jnp.int32),
            pltpu.SemaphoreType.DMA((5, blocks)),
        ],
        compiler_params=pltpu.CompilerParams(vmem_limit_bytes=MATCH_LIMIT * MIB),
    )(table, place, last, slots, slot_meta, cols)


def collect_kernel(found_ref, own_ref, out_ref):
    found = jnp.max(found_ref[...], axis=0, keepdims=True)
    column = jnp.concatenate([turn(found[:, h : h + 256]) for h in (0, 256)], axis=0)
    for half in (0, 128):
        part = slice(half, half + 128)
        mine = iota((CLUSTERS * SLOTS, 128), 0).astype(jnp.float32) == own_ref[1:2, part]
        best = jnp.max(jnp.where(mine, column, LOW), axis=0, keepdims=True)
        out_ref[:, part] = jnp.maximum(best * own_ref[0:1, part], -1.0)


def collect(found, own):
    return pl.pallas_call(
        collect_kernel,
        out_shape=jax.ShapeDtypeStruct((1, ROWS), jnp.float32),
    )(found, own)


def ring(size, step):
    return [(i, (i + step) % size) for i in range(size)]


def per_device(embeddings, cluster_id, member_order):
    mine = (embeddings, cluster_id, member_order)
    width = embeddings.shape[1]
    hold = lax.optimization_barrier
    own = own_call(prepare_kernel, jax.ShapeDtypeStruct((AUG, width), jnp.bfloat16), *mine)
    cols = lax.all_gather(own, "grp", axis=0, tiled=True)

    up = lambda v: lax.ppermute(v, "span", ring(8, 1))
    down = lambda v: lax.ppermute(v, "span", ring(8, -1))
    u1, d1 = up(own), down(own)
    known = own_call(remember_kernel, jax.ShapeDtypeStruct((2, ROWS), jnp.float32), *mine)
    u1, known = hold((u1, known))
    u2, d2 = up(u1), down(d1)
    u3, d3 = up(u2), down(d2)
    u4 = up(u3)
    place = lax.axis_index("span").astype(jnp.int32).reshape(1)
    slots, slot_meta = spread(place, [own, u1, d1, u2, d2, u3, d3], (0, 7, 1, 6, 2, 5, 3))

    tables = cols.reshape(16, AUG, width)[:, ROWS + START, 0:CLUSTERS].astype(jnp.int32)
    found = match(tables, place, u4, 4, slots, slot_meta, cols).reshape(CLUSTERS, 8, SLOTS)
    found = found.transpose(1, 0, 2).reshape(8, CLUSTERS * SLOTS)
    arrived = lax.all_to_all(found, "span", split_axis=0, concat_axis=0, tiled=True)
    return collect(arrived, known)[0]


def solution(mesh):
    return jax.shard_map(
        per_device,
        mesh=mesh,
        in_specs=(
            P(("outer", "grp", "span"), None),
            P(("outer", "grp", "span")),
            P(("outer", "grp", "span")),
        ),
        out_specs=P(("outer", "grp", "span")),
        check_vma=False,
    )
```

```python
import functools

import jax
import jax.numpy as jnp
from jax import lax
from jax.experimental import pallas as pl
from jax.experimental.pallas import tpu as pltpu
from jax.sharding import Mesh
from jax.sharding import PartitionSpec as P

ROWS = 256
CLUSTERS = 16
SLOTS = 32
WINDOW = 48
ORDERS = 32768.0
LOW = -1e30
HIGH = 1e9
MIB = 1024 * 1024
META = 16
AUG = ROWS + META
START = 7


def iota(shape, dimension):
    return lax.broadcasted_iota(jnp.int32, shape, dimension)


def turn(line):
    return jnp.concatenate([jnp.broadcast_to(line[:, h : h + 128], (128, 128)).T for h in (0, 128)], axis=0)


def tall(meta):
    filled = jnp.concatenate([meta, jnp.zeros((128 - META, ROWS), meta.dtype)], axis=0)
    return jnp.concatenate([filled[:, 0:128].T, filled[:, 128:256].T], axis=0)


def row_facts(rows, cluster, order):
    wide = rows.astype(jnp.float32)
    norm = jnp.broadcast_to(lax.rsqrt(jnp.sum(wide * wide, axis=1, keepdims=True) + 1e-06), (ROWS, 128))
    norm = jnp.concatenate([norm[0:128, :].T[0:1, :], norm[128:256, :].T[0:1, :]], axis=1)
    floor = cluster * ORDERS
    key = floor + order
    key_down = jnp.concatenate([turn(key)] * 2, axis=1)
    rank = jnp.sum((key_down < key).astype(jnp.float32), axis=0, keepdims=True)
    inside = rank - jnp.sum((key_down < floor).astype(jnp.float32), axis=0, keepdims=True)
    return norm, rank, inside


def staged(refs, held, sem):
    copies = [pltpu.make_async_copy(ref, to, sem.at[i]) for i, (ref, to) in enumerate(zip(refs, held))]
    for copy in copies:
        copy.start()
    for copy in copies:
        copy.wait()


def prepare_kernel(x_hbm, cluster_hbm, order_hbm, aug_ref, x_ref, cluster_ref, order_ref, sem):
    staged((x_hbm, cluster_hbm, order_hbm), (x_ref, cluster_ref, order_ref), sem)
    rows = x_ref[...]
    cluster = cluster_ref[...].astype(jnp.float32)
    order = order_ref[...]
    norm, rank, inside = row_facts(rows, cluster, order.astype(jnp.float32))
    high = jnp.right_shift(order, 8).astype(jnp.float32)
    low = jnp.bitwise_and(order, 255).astype(jnp.float32)
    first = norm.astype(jnp.bfloat16).astype(jnp.float32)
    second = (norm - first).astype(jnp.bfloat16).astype(jnp.float32)
    third = norm - first - second

    line = iota((META, ROWS), 0)
    meta = jnp.zeros((META, ROWS), jnp.float32)
    for index, values in enumerate((cluster, high, low, first, second, third, inside)):
        meta = jnp.where(line == index, values, meta)
    permute = (iota((ROWS, ROWS), 0).astype(jnp.float32) == rank).astype(jnp.bfloat16)
    meta = by_lines(meta.astype(jnp.bfloat16), permute)
    count = jnp.sum((turn(cluster) < iota((ROWS, 128), 1).astype(jnp.float32)).astype(jnp.float32), axis=0, keepdims=True)
    start = jnp.minimum(jnp.bitwise_and(count.astype(jnp.int32), -16), ROWS - WINDOW).astype(jnp.float32)
    meta = jnp.where(line == START, jnp.concatenate([start] * 2, axis=1), meta)

    aug_ref[0:ROWS, :] = jnp.dot(permute, rows, preferred_element_type=jnp.float32).astype(jnp.bfloat16)
    aug_ref[ROWS:AUG, :] = jnp.zeros((META, rows.shape[1]), jnp.bfloat16)
    aug_ref[ROWS:AUG, 0:ROWS] = meta.astype(jnp.bfloat16)


def remember_kernel(x_hbm, cluster_hbm, order_hbm, out_ref, x_ref, cluster_ref, order_ref, sem):
    staged((x_hbm, cluster_hbm, order_hbm), (x_ref, cluster_ref, order_ref), sem)
    cluster = cluster_ref[...].astype(jnp.float32)
    norm, _, inside = row_facts(x_ref[...], cluster, order_ref[...].astype(jnp.float32))
    out_ref[0:1, :] = norm
    out_ref[1:2, :] = cluster * float(SLOTS) + inside


def own_call(kernel, out, x, cluster, order):
    return pl.pallas_call(
        kernel,
        out_shape=out,
        in_specs=[pl.BlockSpec(memory_space=pltpu.HBM)] * 3,
        scratch_shapes=[
            pltpu.VMEM(x.shape, x.dtype),
            pltpu.VMEM((1, ROWS), jnp.int32),
            pltpu.VMEM((1, ROWS), jnp.int32),
            pltpu.SemaphoreType.DMA((3,)),
        ],
        compiler_params=pltpu.CompilerParams(vmem_limit_bytes=OWN_LIMIT * MIB),
    )(x, cluster.reshape(1, ROWS), order.reshape(1, ROWS))


def line_weights():
    line, lane = iota((16, 128), 0), iota((16, 128), 1)
    weights = jnp.zeros((16, 128), jnp.float32)
    for at, of, weight in ((0, 0, ORDERS), (0, 1, 256.0), (0, 2, 1.0)):
        weights = jnp.where((line == at) & (lane == of), weight, weights)
    return weights.astype(jnp.bfloat16)


def spread_weights():
    line, lane = iota((128, 256), 0), iota((128, 256), 1)
    weights = jnp.zeros((128, 256), jnp.float32)
    for of, weight in ((0, ORDERS), (1, 256.0), (2, 1.0)):
        weights = jnp.where((line == of) & (lane < 128), weight, weights)
    return jnp.where((line >= 3) & (line <= 5) & (lane >= 128), 1.0, weights).astype(jnp.bfloat16)


def by_lines(weights, meta):
    return lax.dot_general(weights, meta, (((1,), (1,)), ((), ())), preferred_element_type=jnp.float32)


def into_slots(rows, meta):
    wide = meta.astype(jnp.float32)
    slot = wide[0:1] * float(SLOTS) + wide[6:7]
    pick = (iota((CLUSTERS * SLOTS, ROWS), 0).astype(jnp.float32) == slot).astype(jnp.bfloat16)
    both = [jnp.dot(pick, v, preferred_element_type=jnp.float32).astype(jnp.bfloat16) for v in (rows, tall(meta))]
    return [v.reshape(CLUSTERS, SLOTS, v.shape[1]) for v in both]


def home(place_ref, offset):
    return pl.ds(pl.multiple_of(lax.rem(place_ref[0] + offset, 8) * SLOTS, SLOTS), SLOTS)


def spread_kernel(offsets, place_ref, *refs):
    slots, slot_meta = refs[-2:]
    for ref, offset in zip(refs, offsets):
        at = home(place_ref, offset)
        slots[:, at, :], slot_meta[:, at, :] = into_slots(ref[0:ROWS, :], ref[ROWS:AUG, 0:ROWS])


def spread(place, rows, offsets):
    vmem, smem = pl.BlockSpec(memory_space=pltpu.VMEM), pl.BlockSpec(memory_space=pltpu.SMEM)
    width = rows[0].shape[1]
    return pl.pallas_call(
        functools.partial(spread_kernel, offsets),
        out_shape=(
            jax.ShapeDtypeStruct((CLUSTERS, 8 * SLOTS, width), jnp.bfloat16),
            jax.ShapeDtypeStruct((CLUSTERS, 8 * SLOTS, 128), jnp.bfloat16),
        ),
        in_specs=[smem] + [vmem] * len(rows),
        out_specs=(vmem, vmem),
        compiler_params=pltpu.CompilerParams(vmem_limit_bytes=24 * MIB),
    )(place, *rows)


OWN_LIMIT = 56
MATCH_LIMIT = 52
TOP = 144
TEAM = 4


def match_kernel(
    offset, place_ref, last_ref, slots_hbm, slot_meta_hbm, cols_hbm, out_ref,
    held, held_lanes, slots, slot_meta, slot_lines, last_slots, last_meta, starts_vmem, table_ref, waited, sem,
):
    blocks = cols_hbm.shape[0] // AUG

    def part(b, first, last, kind):
        source = cols_hbm.at[b * AUG + first : b * AUG + last, :]
        return pltpu.make_async_copy(source, held.at[b, first:last, :], sem.at[kind, b])

    def team(k):
        at = pl.ds(k * TEAM, TEAM)
        return pltpu.make_async_copy(slots_hbm.at[at], slots.at[at], sem.at[3, k])

    notes = [part(b, ROWS, AUG, 0) for b in range(blocks)]
    tops = [part(b, 0, TOP, 1) for b in range(blocks)]
    rests = [part(b, TOP, ROWS, 2) for b in range(blocks)]
    small = pltpu.make_async_copy(slot_meta_hbm, slot_meta, sem.at[4, 0])
    for copy in [*notes, small]:
        copy.start()
    waited[0] = 0
    last_slots[...], last_meta[...] = into_slots(last_ref[0:ROWS, :], last_ref[ROWS:AUG, 0:ROWS])
    weights = spread_weights()
    for copy in notes:
        copy.wait()
    for copy in [*tops, team(0)]:
        copy.start()
    for b in range(blocks):
        meta = tall(held[b, ROWS:AUG, 0:ROWS])
        held_lanes[b] = jnp.dot(meta, weights, preferred_element_type=jnp.float32)
        starts_vmem[b : b + 1, :] = held[b, ROWS:AUG, 0:128].astype(jnp.float32)[START : START + 1].astype(jnp.int32)
    table = pltpu.make_async_copy(starts_vmem, table_ref, sem.at[4, 1])
    table.start()
    at = home(place_ref, offset)
    small.wait()
    slot_meta[:, at, :] = last_meta[...]
    weights = line_weights()
    for g in range(CLUSTERS):
        slot_lines[g] = by_lines(weights, slot_meta[g])[0:8]
    table.wait()
    for copy in tops:
        copy.wait()
    for copy in rests:
        copy.start()
    groups = blocks * WINDOW // 8

    def cluster(g):
        starts = [pl.multiple_of(table_ref[b, g], 16) for b in range(blocks)]
        window = jnp.concatenate([held[b, pl.ds(starts[b], WINDOW), :] for b in range(blocks)], axis=0)
        lanes = jnp.concatenate([held_lanes[b, pl.ds(starts[b], WINDOW), :] for b in range(blocks)], axis=0)
        score = by_lines(window, slots[g])
        key = lanes[:, 0:128]
        key = jnp.where(key >= (g * int(ORDERS)).astype(jnp.float32), key, HIGH).reshape(groups, 8, 128)
        norm = lanes[:, 128:256].reshape(groups, 8, 128)
        halves = []
        for half in (0, 128):
            valid = key < slot_lines[g, 0:1, half : half + 128]
            scaled = score[:, half : half + 128].reshape(groups, 8, 128) * norm
            halves.append(jnp.max(jnp.where(valid, scaled, LOW), axis=0))
        best = jnp.concatenate(halves, axis=1)
        out_ref[g] = jnp.max(best, axis=0, keepdims=True)

    def step(k, carry):
        @pl.when(k + 1 < CLUSTERS // TEAM)
        def _():
            team(k + 1).start()

        end = functools.reduce(jnp.maximum, [table_ref[b, k * TEAM + TEAM - 1] for b in range(blocks)]) + WINDOW

        @pl.when((waited[0] == 0) & ((end > TOP) | (k == CLUSTERS // TEAM - 1)))
        def _():
            for copy in rests:
                copy.wait()
            waited[0] = 1

        team(k).wait()
        of = pl.ds(k * TEAM, TEAM)
        slots[of, at, :] = last_slots[of]
        for i in range(TEAM):
            cluster(k * TEAM + i)
        return carry

    lax.fori_loop(0, CLUSTERS // TEAM, step, 0)


def match(place, last, offset, slots, slot_meta, cols):
    width = cols.shape[1]
    blocks = cols.shape[0] // AUG
    vmem, smem = pl.BlockSpec(memory_space=pltpu.VMEM), pl.BlockSpec(memory_space=pltpu.SMEM)
    hbm = pl.BlockSpec(memory_space=pltpu.HBM)
    return pl.pallas_call(
        functools.partial(match_kernel, offset),
        out_shape=jax.ShapeDtypeStruct((CLUSTERS, 1, 8 * SLOTS), jnp.float32),
        in_specs=[smem, vmem, hbm, hbm, hbm],
        out_specs=vmem,
        scratch_shapes=[
            pltpu.VMEM((blocks, AUG, width), jnp.bfloat16),
            pltpu.VMEM((blocks, ROWS, 256), jnp.float32),
            pltpu.VMEM((CLUSTERS, 8 * SLOTS, width), jnp.bfloat16),
            pltpu.VMEM((CLUSTERS, 8 * SLOTS, 128), jnp.bfloat16),
            pltpu.VMEM((CLUSTERS, 8, 8 * SLOTS), jnp.float32),
            pltpu.VMEM((CLUSTERS, SLOTS, width), jnp.bfloat16),
            pltpu.VMEM((CLUSTERS, SLOTS, 128), jnp.bfloat16),
            pltpu.VMEM((blocks, 128), jnp.int32),
            pltpu.SMEM((blocks, 128), jnp.int32),
            pltpu.SMEM((1,), jnp.int32),
            pltpu.SemaphoreType.DMA((5, blocks)),
        ],
        compiler_params=pltpu.CompilerParams(vmem_limit_bytes=MATCH_LIMIT * MIB),
    )(place, last, slots, slot_meta, cols)


def collect_kernel(found_ref, own_ref, out_ref):
    found = jnp.max(found_ref[...], axis=0)
    column = jnp.concatenate([turn(found[:, h : h + 256]) for h in (0, 256)], axis=0)
    for half in (0, 128):
        part = slice(half, half + 128)
        mine = iota((CLUSTERS * SLOTS, 128), 0).astype(jnp.float32) == own_ref[1:2, part]
        best = jnp.max(jnp.where(mine, column, LOW), axis=0, keepdims=True)
        out_ref[:, part] = jnp.maximum(best * own_ref[0:1, part], -1.0)


def collect(found, own):
    return pl.pallas_call(
        collect_kernel,
        out_shape=jax.ShapeDtypeStruct((1, ROWS), jnp.float32),
    )(found, own)


def ring(size, step):
    return [(i, (i + step) % size) for i in range(size)]


def per_device(embeddings, cluster_id, member_order):
    mine = (embeddings, cluster_id, member_order)
    width = embeddings.shape[1]
    hold = lax.optimization_barrier
    own = own_call(prepare_kernel, jax.ShapeDtypeStruct((AUG, width), jnp.bfloat16), *mine)
    cols = lax.all_gather(own, ("z", "core"), axis=0, tiled=True)

    up = lambda v: lax.ppermute(v, "y", ring(8, 1))
    down = lambda v: lax.ppermute(v, "y", ring(8, -1))
    u1, d1 = up(own), down(own)
    known = own_call(remember_kernel, jax.ShapeDtypeStruct((2, ROWS), jnp.float32), *mine)
    u1, known = hold((u1, known))
    u2, d2 = up(u1), down(d1)
    u3, d3 = up(u2), down(d2)
    u4 = up(u3)
    place = lax.axis_index("y").astype(jnp.int32).reshape(1)
    slots, slot_meta = spread(place, [own, u1, d1, u2, d2, u3, d3], (0, 7, 1, 6, 2, 5, 3))

    found = match(place, u4, 4, slots, slot_meta, cols).reshape(CLUSTERS, 8, SLOTS)
    found = found.transpose(1, 0, 2).reshape(8, 1, CLUSTERS * SLOTS)
    arrived = lax.all_to_all(found, "y", split_axis=0, concat_axis=0, tiled=True)
    return collect(arrived, known)[0]


def solution(mesh):
    axes = ("x", "z", "core", "y")
    finer = Mesh(mesh.devices.reshape(mesh.shape["outer"], 8, 2, 8), axes)
    return jax.shard_map(
        per_device,
        mesh=finer,
        in_specs=(P(axes, None), P(axes), P(axes)),
        out_specs=P(axes),
        check_vma=False,
    )
```

```python
import functools

import jax
import jax.numpy as jnp
from jax import lax
from jax.experimental import pallas as pl
from jax.experimental.pallas import tpu as pltpu
from jax.sharding import Mesh
from jax.sharding import PartitionSpec as P

ROWS = 256
CLUSTERS = 16
SLOTS = 32
WINDOW = 48
ORDERS = 32768.0
LOW = -1e30
HIGH = 1e9
MIB = 1024 * 1024
META = 16
AUG = ROWS + META
START = 7


def iota(shape, dimension):
    return lax.broadcasted_iota(jnp.int32, shape, dimension)


def turn(line):
    return jnp.concatenate([jnp.broadcast_to(line[:, h : h + 128], (128, 128)).T for h in (0, 128)], axis=0)


def tall(meta):
    filled = jnp.concatenate([meta, jnp.zeros((128 - META, ROWS), meta.dtype)], axis=0)
    return jnp.concatenate([filled[:, 0:128].T, filled[:, 128:256].T], axis=0)


def row_facts(rows, cluster, order):
    wide = rows.astype(jnp.float32)
    norm = jnp.broadcast_to(lax.rsqrt(jnp.sum(wide * wide, axis=1, keepdims=True) + 1e-06), (ROWS, 128))
    norm = jnp.concatenate([norm[0:128, :].T[0:1, :], norm[128:256, :].T[0:1, :]], axis=1)
    floor = cluster * ORDERS
    key = floor + order
    key_down = jnp.concatenate([turn(key)] * 2, axis=1)
    rank = jnp.sum((key_down < key).astype(jnp.float32), axis=0, keepdims=True)
    inside = rank - jnp.sum((key_down < floor).astype(jnp.float32), axis=0, keepdims=True)
    return norm, rank, inside


def staged(refs, held, sem):
    copies = [pltpu.make_async_copy(ref, to, sem.at[i]) for i, (ref, to) in enumerate(zip(refs, held))]
    for copy in copies:
        copy.start()
    for copy in copies:
        copy.wait()


def prepare_kernel(x_hbm, cluster_hbm, order_hbm, aug_ref, x_ref, cluster_ref, order_ref, sem):
    staged((x_hbm, cluster_hbm, order_hbm), (x_ref, cluster_ref, order_ref), sem)
    rows = x_ref[...]
    cluster = cluster_ref[...].astype(jnp.float32)
    order = order_ref[...]
    norm, rank, inside = row_facts(rows, cluster, order.astype(jnp.float32))
    high = jnp.right_shift(order, 8).astype(jnp.float32)
    low = jnp.bitwise_and(order, 255).astype(jnp.float32)
    first = norm.astype(jnp.bfloat16).astype(jnp.float32)
    second = (norm - first).astype(jnp.bfloat16).astype(jnp.float32)
    third = norm - first - second

    line = iota((META, ROWS), 0)
    meta = jnp.zeros((META, ROWS), jnp.float32)
    for index, values in enumerate((cluster, high, low, first, second, third, inside)):
        meta = jnp.where(line == index, values, meta)
    permute = (iota((ROWS, ROWS), 0).astype(jnp.float32) == rank).astype(jnp.bfloat16)
    meta = by_lines(meta.astype(jnp.bfloat16), permute)
    count = jnp.sum((turn(cluster) < iota((ROWS, 128), 1).astype(jnp.float32)).astype(jnp.float32), axis=0, keepdims=True)
    start = jnp.minimum(jnp.bitwise_and(count.astype(jnp.int32), -16), ROWS - WINDOW).astype(jnp.float32)
    meta = jnp.where(line == START, jnp.concatenate([start] * 2, axis=1), meta)

    aug_ref[0:ROWS, :] = jnp.dot(permute, rows, preferred_element_type=jnp.float32).astype(jnp.bfloat16)
    aug_ref[ROWS:AUG, :] = jnp.zeros((META, rows.shape[1]), jnp.bfloat16)
    aug_ref[ROWS:AUG, 0:ROWS] = meta.astype(jnp.bfloat16)


def remember_kernel(x_hbm, cluster_hbm, order_hbm, out_ref, x_ref, cluster_ref, order_ref, sem):
    staged((x_hbm, cluster_hbm, order_hbm), (x_ref, cluster_ref, order_ref), sem)
    cluster = cluster_ref[...].astype(jnp.float32)
    norm, _, inside = row_facts(x_ref[...], cluster, order_ref[...].astype(jnp.float32))
    out_ref[0:1, :] = norm
    out_ref[1:2, :] = cluster * float(SLOTS) + inside


def own_call(kernel, out, x, cluster, order):
    return pl.pallas_call(
        kernel,
        out_shape=out,
        in_specs=[pl.BlockSpec(memory_space=pltpu.HBM)] * 3,
        scratch_shapes=[
            pltpu.VMEM(x.shape, x.dtype),
            pltpu.VMEM((1, ROWS), jnp.int32),
            pltpu.VMEM((1, ROWS), jnp.int32),
            pltpu.SemaphoreType.DMA((3,)),
        ],
        compiler_params=pltpu.CompilerParams(vmem_limit_bytes=OWN_LIMIT * MIB),
    )(x, cluster.reshape(1, ROWS), order.reshape(1, ROWS))


def line_weights():
    line, lane = iota((16, 128), 0), iota((16, 128), 1)
    weights = jnp.zeros((16, 128), jnp.float32)
    for at, of, weight in ((0, 0, ORDERS), (0, 1, 256.0), (0, 2, 1.0)):
        weights = jnp.where((line == at) & (lane == of), weight, weights)
    return weights.astype(jnp.bfloat16)


def spread_weights():
    line, lane = iota((128, 256), 0), iota((128, 256), 1)
    weights = jnp.zeros((128, 256), jnp.float32)
    for of, weight in ((0, ORDERS), (1, 256.0), (2, 1.0)):
        weights = jnp.where((line == of) & (lane < 128), weight, weights)
    return jnp.where((line >= 3) & (line <= 5) & (lane >= 128), 1.0, weights).astype(jnp.bfloat16)


def by_lines(weights, meta):
    return lax.dot_general(weights, meta, (((1,), (1,)), ((), ())), preferred_element_type=jnp.float32)


def into_slots(rows, meta):
    wide = meta.astype(jnp.float32)
    slot = wide[0:1] * float(SLOTS) + wide[6:7]
    pick = (iota((CLUSTERS * SLOTS, ROWS), 0).astype(jnp.float32) == slot).astype(jnp.bfloat16)
    both = [jnp.dot(pick, v, preferred_element_type=jnp.float32).astype(jnp.bfloat16) for v in (rows, tall(meta))]
    return [v.reshape(CLUSTERS, SLOTS, v.shape[1]) for v in both]


def home(place_ref, offset):
    return pl.ds(pl.multiple_of(lax.rem(place_ref[0] + offset, 8) * SLOTS, SLOTS), SLOTS)


def spread_kernel(offsets, place_ref, *refs):
    slots, slot_meta = refs[-2:]
    for ref, offset in zip(refs, offsets):
        at = home(place_ref, offset)
        slots[:, at, :], slot_meta[:, at, :] = into_slots(ref[0:ROWS, :], ref[ROWS:AUG, 0:ROWS])


def spread(place, rows, offsets):
    vmem, smem = pl.BlockSpec(memory_space=pltpu.VMEM), pl.BlockSpec(memory_space=pltpu.SMEM)
    width = rows[0].shape[1]
    return pl.pallas_call(
        functools.partial(spread_kernel, offsets),
        out_shape=(
            jax.ShapeDtypeStruct((CLUSTERS, 8 * SLOTS, width), jnp.bfloat16),
            jax.ShapeDtypeStruct((CLUSTERS, 8 * SLOTS, 128), jnp.bfloat16),
        ),
        in_specs=[smem] + [vmem] * len(rows),
        out_specs=(vmem, vmem),
        compiler_params=pltpu.CompilerParams(vmem_limit_bytes=24 * MIB),
    )(place, *rows)


OWN_LIMIT = 56
MATCH_LIMIT = 52
TOP = 144
TEAM = 4


def match_kernel(
    offset, place_ref, last_ref, slots_hbm, slot_meta_hbm, cols_hbm, out_ref,
    held, held_lanes, slots, slot_meta, slot_lines, last_slots, last_meta, starts_vmem, table_ref, waited, sem,
):
    blocks = cols_hbm.shape[0] // AUG

    def part(b, first, last, kind):
        source = cols_hbm.at[b * AUG + first : b * AUG + last, :]
        return pltpu.make_async_copy(source, held.at[b, first:last, :], sem.at[kind, b])

    def team(k):
        at = pl.ds(k * TEAM, TEAM)
        return pltpu.make_async_copy(slots_hbm.at[at], slots.at[at], sem.at[3, k])

    notes = [part(b, ROWS, AUG, 0) for b in range(blocks)]
    tops = [part(b, 0, TOP, 1) for b in range(blocks)]
    rests = [part(b, TOP, ROWS, 2) for b in range(blocks)]
    small = pltpu.make_async_copy(slot_meta_hbm, slot_meta, sem.at[4, 0])
    for copy in [*notes, small]:
        copy.start()
    waited[0] = 0
    last_slots[...], last_meta[...] = into_slots(last_ref[0:ROWS, :], last_ref[ROWS:AUG, 0:ROWS])
    weights = spread_weights()
    for copy in [*tops, team(0), *rests]:
        copy.start()
    for copy in notes:
        copy.wait()
    for b in range(blocks):
        meta = tall(held[b, ROWS:AUG, 0:ROWS])
        held_lanes[b] = jnp.dot(meta, weights, preferred_element_type=jnp.float32)
        starts_vmem[b : b + 1, :] = held[b, ROWS:AUG, 0:128].astype(jnp.float32)[START : START + 1].astype(jnp.int32)
    table = pltpu.make_async_copy(starts_vmem, table_ref, sem.at[4, 1])
    table.start()
    at = home(place_ref, offset)
    small.wait()
    slot_meta[:, at, :] = last_meta[...]
    weights = line_weights()
    for g in range(CLUSTERS):
        slot_lines[g] = by_lines(weights, slot_meta[g])[0:8]
    table.wait()
    for copy in tops:
        copy.wait()
    groups = blocks * WINDOW // 8

    def cluster(g):
        starts = [pl.multiple_of(table_ref[b, g], 16) for b in range(blocks)]
        window = jnp.concatenate([held[b, pl.ds(starts[b], WINDOW), :] for b in range(blocks)], axis=0)
        lanes = jnp.concatenate([held_lanes[b, pl.ds(starts[b], WINDOW), :] for b in range(blocks)], axis=0)
        score = by_lines(window, slots[g])
        key = lanes[:, 0:128]
        key = jnp.where(key >= (g * int(ORDERS)).astype(jnp.float32), key, HIGH).reshape(groups, 8, 128)
        norm = lanes[:, 128:256].reshape(groups, 8, 128)
        halves = []
        for half in (0, 128):
            valid = key < slot_lines[g, 0:1, half : half + 128]
            scaled = score[:, half : half + 128].reshape(groups, 8, 128) * norm
            halves.append(jnp.max(jnp.where(valid, scaled, LOW), axis=0))
        best = jnp.concatenate(halves, axis=1)
        out_ref[g] = jnp.max(best, axis=0, keepdims=True)

    def step(k, carry):
        @pl.when(k + 1 < CLUSTERS // TEAM)
        def _():
            team(k + 1).start()

        end = functools.reduce(jnp.maximum, [table_ref[b, k * TEAM + TEAM - 1] for b in range(blocks)]) + WINDOW

        @pl.when((waited[0] == 0) & ((end > TOP) | (k == CLUSTERS // TEAM - 1)))
        def _():
            for copy in rests:
                copy.wait()
            waited[0] = 1

        team(k).wait()
        of = pl.ds(k * TEAM, TEAM)
        slots[of, at, :] = last_slots[of]
        for i in range(TEAM):
            cluster(k * TEAM + i)
        return carry

    lax.fori_loop(0, CLUSTERS // TEAM, step, 0)


def match(place, last, offset, slots, slot_meta, cols):
    width = cols.shape[1]
    blocks = cols.shape[0] // AUG
    vmem, smem = pl.BlockSpec(memory_space=pltpu.VMEM), pl.BlockSpec(memory_space=pltpu.SMEM)
    hbm = pl.BlockSpec(memory_space=pltpu.HBM)
    return pl.pallas_call(
        functools.partial(match_kernel, offset),
        out_shape=jax.ShapeDtypeStruct((CLUSTERS, 1, 8 * SLOTS), jnp.float32),
        in_specs=[smem, vmem, hbm, hbm, hbm],
        out_specs=vmem,
        scratch_shapes=[
            pltpu.VMEM((blocks, AUG, width), jnp.bfloat16),
            pltpu.VMEM((blocks, ROWS, 256), jnp.float32),
            pltpu.VMEM((CLUSTERS, 8 * SLOTS, width), jnp.bfloat16),
            pltpu.VMEM((CLUSTERS, 8 * SLOTS, 128), jnp.bfloat16),
            pltpu.VMEM((CLUSTERS, 8, 8 * SLOTS), jnp.float32),
            pltpu.VMEM((CLUSTERS, SLOTS, width), jnp.bfloat16),
            pltpu.VMEM((CLUSTERS, SLOTS, 128), jnp.bfloat16),
            pltpu.VMEM((blocks, 128), jnp.int32),
            pltpu.SMEM((blocks, 128), jnp.int32),
            pltpu.SMEM((1,), jnp.int32),
            pltpu.SemaphoreType.DMA((5, blocks)),
        ],
        compiler_params=pltpu.CompilerParams(vmem_limit_bytes=MATCH_LIMIT * MIB),
    )(place, last, slots, slot_meta, cols)


def collect_kernel(found_ref, own_ref, out_ref):
    found = jnp.max(found_ref[...], axis=0)
    column = jnp.concatenate([turn(found[:, h : h + 256]) for h in (0, 256)], axis=0)
    for half in (0, 128):
        part = slice(half, half + 128)
        mine = iota((CLUSTERS * SLOTS, 128), 0).astype(jnp.float32) == own_ref[1:2, part]
        best = jnp.max(jnp.where(mine, column, LOW), axis=0, keepdims=True)
        out_ref[:, part] = jnp.maximum(best * own_ref[0:1, part], -1.0)


def collect(found, own):
    return pl.pallas_call(
        collect_kernel,
        out_shape=jax.ShapeDtypeStruct((1, ROWS), jnp.float32),
    )(found, own)


def ring(size, step):
    return [(i, (i + step) % size) for i in range(size)]


def per_device(embeddings, cluster_id, member_order):
    mine = (embeddings, cluster_id, member_order)
    width = embeddings.shape[1]
    hold = lax.optimization_barrier
    own = own_call(prepare_kernel, jax.ShapeDtypeStruct((AUG, width), jnp.bfloat16), *mine)
    cols = lax.all_gather(own, ("z", "core"), axis=0, tiled=True)

    up = lambda v: lax.ppermute(v, "y", ring(8, 1))
    down = lambda v: lax.ppermute(v, "y", ring(8, -1))
    u1, d1 = up(own), down(own)
    known = own_call(remember_kernel, jax.ShapeDtypeStruct((2, ROWS), jnp.float32), *mine)
    u1, known = hold((u1, known))
    u2, d2 = up(u1), down(d1)
    u3, d3 = up(u2), down(d2)
    u4 = up(u3)
    place = lax.axis_index("y").astype(jnp.int32).reshape(1)
    slots, slot_meta = spread(place, [own, u1, d1, u2, d2, u3, d3], (0, 7, 1, 6, 2, 5, 3))

    found = match(place, u4, 4, slots, slot_meta, cols).reshape(CLUSTERS, 8, SLOTS)
    found = found.transpose(1, 0, 2).reshape(8, 1, CLUSTERS * SLOTS)
    arrived = lax.all_to_all(found, "y", split_axis=0, concat_axis=0, tiled=True)
    return collect(arrived, known)[0]


def solution(mesh):
    axes = ("x", "z", "core", "y")
    finer = Mesh(mesh.devices.reshape(mesh.shape["outer"], 8, 2, 8), axes)
    return jax.shard_map(
        per_device,
        mesh=finer,
        in_specs=(P(axes, None), P(axes), P(axes)),
        out_specs=P(axes),
        check_vma=False,
    )
```

```python
import functools

import jax
import jax.numpy as jnp
from jax import lax
from jax.experimental import pallas as pl
from jax.experimental.pallas import tpu as pltpu
from jax.sharding import Mesh
from jax.sharding import PartitionSpec as P

ROWS = 256
CLUSTERS = 16
SLOTS = 32
WINDOW = 48
ORDERS = 32768.0
LOW = -1e30
HIGH = 1e9
MIB = 1024 * 1024
META = 16
AUG = ROWS + META
START = 7


def iota(shape, dimension):
    return lax.broadcasted_iota(jnp.int32, shape, dimension)


def turn(line):
    return jnp.concatenate([jnp.broadcast_to(line[:, h : h + 128], (128, 128)).T for h in (0, 128)], axis=0)


def tall(meta):
    filled = jnp.concatenate([meta, jnp.zeros((128 - META, ROWS), meta.dtype)], axis=0)
    return jnp.concatenate([filled[:, 0:128].T, filled[:, 128:256].T], axis=0)


def row_facts(rows, cluster, order):
    wide = rows.astype(jnp.float32)
    norm = jnp.broadcast_to(lax.rsqrt(jnp.sum(wide * wide, axis=1, keepdims=True) + 1e-06), (ROWS, 128))
    norm = jnp.concatenate([norm[0:128, :].T[0:1, :], norm[128:256, :].T[0:1, :]], axis=1)
    floor = cluster * ORDERS
    key = floor + order
    key_down = jnp.concatenate([turn(key)] * 2, axis=1)
    rank = jnp.sum((key_down < key).astype(jnp.float32), axis=0, keepdims=True)
    inside = rank - jnp.sum((key_down < floor).astype(jnp.float32), axis=0, keepdims=True)
    return norm, rank, inside


def staged(refs, held, sem):
    copies = [pltpu.make_async_copy(ref, to, sem.at[i]) for i, (ref, to) in enumerate(zip(refs, held))]
    for copy in copies:
        copy.start()
    for copy in copies:
        copy.wait()


def prepare_kernel(x_hbm, cluster_hbm, order_hbm, aug_ref, x_ref, cluster_ref, order_ref, sem):
    staged((x_hbm, cluster_hbm, order_hbm), (x_ref, cluster_ref, order_ref), sem)
    rows = x_ref[...]
    cluster = cluster_ref[...].astype(jnp.float32)
    order = order_ref[...]
    norm, rank, inside = row_facts(rows, cluster, order.astype(jnp.float32))
    high = jnp.right_shift(order, 8).astype(jnp.float32)
    low = jnp.bitwise_and(order, 255).astype(jnp.float32)
    first = norm.astype(jnp.bfloat16).astype(jnp.float32)
    second = (norm - first).astype(jnp.bfloat16).astype(jnp.float32)
    third = norm - first - second

    line = iota((META, ROWS), 0)
    meta = jnp.zeros((META, ROWS), jnp.float32)
    for index, values in enumerate((cluster, high, low, first, second, third, inside)):
        meta = jnp.where(line == index, values, meta)
    permute = (iota((ROWS, ROWS), 0).astype(jnp.float32) == rank).astype(jnp.bfloat16)
    meta = by_lines(meta.astype(jnp.bfloat16), permute)
    count = jnp.sum((turn(cluster) < iota((ROWS, 128), 1).astype(jnp.float32)).astype(jnp.float32), axis=0, keepdims=True)
    start = jnp.minimum(jnp.bitwise_and(count.astype(jnp.int32), -16), ROWS - WINDOW).astype(jnp.float32)
    meta = jnp.where(line == START, jnp.concatenate([start] * 2, axis=1), meta)

    aug_ref[0:ROWS, :] = jnp.dot(permute, rows, preferred_element_type=jnp.float32).astype(jnp.bfloat16)
    aug_ref[ROWS:AUG, :] = jnp.zeros((META, rows.shape[1]), jnp.bfloat16)
    aug_ref[ROWS:AUG, 0:ROWS] = meta.astype(jnp.bfloat16)


def remember_kernel(x_hbm, cluster_hbm, order_hbm, out_ref, x_ref, cluster_ref, order_ref, sem):
    staged((x_hbm, cluster_hbm, order_hbm), (x_ref, cluster_ref, order_ref), sem)
    cluster = cluster_ref[...].astype(jnp.float32)
    norm, _, inside = row_facts(x_ref[...], cluster, order_ref[...].astype(jnp.float32))
    out_ref[0:1, :] = norm
    out_ref[1:2, :] = cluster * float(SLOTS) + inside


def own_call(kernel, out, x, cluster, order):
    return pl.pallas_call(
        kernel,
        out_shape=out,
        in_specs=[pl.BlockSpec(memory_space=pltpu.HBM)] * 3,
        scratch_shapes=[
            pltpu.VMEM(x.shape, x.dtype),
            pltpu.VMEM((1, ROWS), jnp.int32),
            pltpu.VMEM((1, ROWS), jnp.int32),
            pltpu.SemaphoreType.DMA((3,)),
        ],
        compiler_params=pltpu.CompilerParams(vmem_limit_bytes=OWN_LIMIT * MIB),
    )(x, cluster.reshape(1, ROWS), order.reshape(1, ROWS))


def line_weights():
    line, lane = iota((16, 128), 0), iota((16, 128), 1)
    weights = jnp.zeros((16, 128), jnp.float32)
    for at, of, weight in ((0, 0, ORDERS), (0, 1, 256.0), (0, 2, 1.0)):
        weights = jnp.where((line == at) & (lane == of), weight, weights)
    return weights.astype(jnp.bfloat16)


def spread_weights():
    line, lane = iota((128, 256), 0), iota((128, 256), 1)
    weights = jnp.zeros((128, 256), jnp.float32)
    for of, weight in ((0, ORDERS), (1, 256.0), (2, 1.0)):
        weights = jnp.where((line == of) & (lane < 128), weight, weights)
    return jnp.where((line >= 3) & (line <= 5) & (lane >= 128), 1.0, weights).astype(jnp.bfloat16)


def by_lines(weights, meta):
    return lax.dot_general(weights, meta, (((1,), (1,)), ((), ())), preferred_element_type=jnp.float32)


def into_slots(rows, meta):
    wide = meta.astype(jnp.float32)
    slot = wide[0:1] * float(SLOTS) + wide[6:7]
    pick = (iota((CLUSTERS * SLOTS, ROWS), 0).astype(jnp.float32) == slot).astype(jnp.bfloat16)
    both = [jnp.dot(pick, v, preferred_element_type=jnp.float32).astype(jnp.bfloat16) for v in (rows, tall(meta))]
    return [v.reshape(CLUSTERS, SLOTS, v.shape[1]) for v in both]


def home(place_ref, offset):
    return pl.ds(pl.multiple_of(lax.rem(place_ref[0] + offset, 8) * SLOTS, SLOTS), SLOTS)


def spread_kernel(offsets, place_ref, *refs):
    slots, slot_meta = refs[-2:]
    for ref, offset in zip(refs, offsets):
        at = home(place_ref, offset)
        slots[:, at, :], slot_meta[:, at, :] = into_slots(ref[0:ROWS, :], ref[ROWS:AUG, 0:ROWS])


def spread(place, rows, offsets):
    vmem, smem = pl.BlockSpec(memory_space=pltpu.VMEM), pl.BlockSpec(memory_space=pltpu.SMEM)
    width = rows[0].shape[1]
    return pl.pallas_call(
        functools.partial(spread_kernel, offsets),
        out_shape=(
            jax.ShapeDtypeStruct((CLUSTERS, 8 * SLOTS, width), jnp.bfloat16),
            jax.ShapeDtypeStruct((CLUSTERS, 8 * SLOTS, 128), jnp.bfloat16),
        ),
        in_specs=[smem] + [vmem] * len(rows),
        out_specs=(vmem, vmem),
        compiler_params=pltpu.CompilerParams(vmem_limit_bytes=24 * MIB),
    )(place, *rows)


OWN_LIMIT = 56
MATCH_LIMIT = 52
TOP = 144
TEAM = 4


def match_kernel(
    offset, place_ref, last_hbm, slots_hbm, slot_meta_hbm, cols_hbm, out_ref,
    held, held_lanes, slots, slot_meta, slot_lines, last_ref, last_slots, last_meta, starts_vmem, table_ref, waited, sem,
):
    blocks = cols_hbm.shape[0] // AUG

    def part(b, first, last, kind):
        source = cols_hbm.at[b * AUG + first : b * AUG + last, :]
        return pltpu.make_async_copy(source, held.at[b, first:last, :], sem.at[kind, b])

    def team(k):
        at = pl.ds(k * TEAM, TEAM)
        return pltpu.make_async_copy(slots_hbm.at[at], slots.at[at], sem.at[3, k])

    notes = [part(b, ROWS, AUG, 0) for b in range(blocks)]
    tops = [part(b, 0, TOP, 1) for b in range(blocks)]
    rests = [part(b, TOP, ROWS, 2) for b in range(blocks)]
    small = pltpu.make_async_copy(slot_meta_hbm, slot_meta, sem.at[4, 0])
    last = pltpu.make_async_copy(last_hbm, last_ref, sem.at[4, 2])
    for copy in [last, *notes, small]:
        copy.start()
    waited[0] = 0
    last.wait()
    last_slots[...], last_meta[...] = into_slots(last_ref[0:ROWS, :], last_ref[ROWS:AUG, 0:ROWS])
    weights = spread_weights()
    for copy in [*tops, team(0), *rests]:
        copy.start()
    for copy in notes:
        copy.wait()
    for b in range(blocks):
        meta = tall(held[b, ROWS:AUG, 0:ROWS])
        held_lanes[b] = jnp.dot(meta, weights, preferred_element_type=jnp.float32)
        starts_vmem[b : b + 1, :] = held[b, ROWS:AUG, 0:128].astype(jnp.float32)[START : START + 1].astype(jnp.int32)
    table = pltpu.make_async_copy(starts_vmem, table_ref, sem.at[4, 1])
    table.start()
    at = home(place_ref, offset)
    small.wait()
    slot_meta[:, at, :] = last_meta[...]
    weights = line_weights()
    for g in range(CLUSTERS):
        slot_lines[g] = by_lines(weights, slot_meta[g])[0:8]
    table.wait()
    for copy in tops:
        copy.wait()
    groups = blocks * WINDOW // 8

    def cluster(g):
        starts = [pl.multiple_of(table_ref[b, g], 16) for b in range(blocks)]
        window = jnp.concatenate([held[b, pl.ds(starts[b], WINDOW), :] for b in range(blocks)], axis=0)
        lanes = jnp.concatenate([held_lanes[b, pl.ds(starts[b], WINDOW), :] for b in range(blocks)], axis=0)
        score = by_lines(window, slots[g])
        key = lanes[:, 0:128]
        key = jnp.where(key >= (g * int(ORDERS)).astype(jnp.float32), key, HIGH).reshape(groups, 8, 128)
        norm = lanes[:, 128:256].reshape(groups, 8, 128)
        halves = []
        for half in (0, 128):
            valid = key < slot_lines[g, 0:1, half : half + 128]
            scaled = score[:, half : half + 128].reshape(groups, 8, 128) * norm
            halves.append(jnp.max(jnp.where(valid, scaled, LOW), axis=0))
        best = jnp.concatenate(halves, axis=1)
        out_ref[g] = jnp.max(best, axis=0, keepdims=True)

    def step(k, carry):
        @pl.when(k + 1 < CLUSTERS // TEAM)
        def _():
            team(k + 1).start()

        end = functools.reduce(jnp.maximum, [table_ref[b, k * TEAM + TEAM - 1] for b in range(blocks)]) + WINDOW

        @pl.when((waited[0] == 0) & ((end > TOP) | (k == CLUSTERS // TEAM - 1)))
        def _():
            for copy in rests:
                copy.wait()
            waited[0] = 1

        team(k).wait()
        of = pl.ds(k * TEAM, TEAM)
        slots[of, at, :] = last_slots[of]
        for i in range(TEAM):
            cluster(k * TEAM + i)
        return carry

    lax.fori_loop(0, CLUSTERS // TEAM, step, 0)


def match(place, last, offset, slots, slot_meta, cols):
    width = cols.shape[1]
    blocks = cols.shape[0] // AUG
    vmem, smem = pl.BlockSpec(memory_space=pltpu.VMEM), pl.BlockSpec(memory_space=pltpu.SMEM)
    hbm = pl.BlockSpec(memory_space=pltpu.HBM)
    return pl.pallas_call(
        functools.partial(match_kernel, offset),
        out_shape=jax.ShapeDtypeStruct((CLUSTERS, 1, 8 * SLOTS), jnp.float32),
        in_specs=[smem, hbm, hbm, hbm, hbm],
        out_specs=vmem,
        scratch_shapes=[
            pltpu.VMEM((blocks, AUG, width), jnp.bfloat16),
            pltpu.VMEM((blocks, ROWS, 256), jnp.float32),
            pltpu.VMEM((CLUSTERS, 8 * SLOTS, width), jnp.bfloat16),
            pltpu.VMEM((CLUSTERS, 8 * SLOTS, 128), jnp.bfloat16),
            pltpu.VMEM((CLUSTERS, 8, 8 * SLOTS), jnp.float32),
            pltpu.VMEM((AUG, width), jnp.bfloat16),
            pltpu.VMEM((CLUSTERS, SLOTS, width), jnp.bfloat16),
            pltpu.VMEM((CLUSTERS, SLOTS, 128), jnp.bfloat16),
            pltpu.VMEM((blocks, 128), jnp.int32),
            pltpu.SMEM((blocks, 128), jnp.int32),
            pltpu.SMEM((1,), jnp.int32),
            pltpu.SemaphoreType.DMA((5, blocks)),
        ],
        compiler_params=pltpu.CompilerParams(vmem_limit_bytes=MATCH_LIMIT * MIB),
    )(place, last, slots, slot_meta, cols)


def collect_kernel(found_ref, own_ref, out_ref):
    found = jnp.max(found_ref[...], axis=0)
    column = jnp.concatenate([turn(found[:, h : h + 256]) for h in (0, 256)], axis=0)
    for half in (0, 128):
        part = slice(half, half + 128)
        mine = iota((CLUSTERS * SLOTS, 128), 0).astype(jnp.float32) == own_ref[1:2, part]
        best = jnp.max(jnp.where(mine, column, LOW), axis=0, keepdims=True)
        out_ref[:, part] = jnp.maximum(best * own_ref[0:1, part], -1.0)


def collect(found, own):
    return pl.pallas_call(
        collect_kernel,
        out_shape=jax.ShapeDtypeStruct((1, ROWS), jnp.float32),
    )(found, own)


def ring(size, step):
    return [(i, (i + step) % size) for i in range(size)]


def per_device(embeddings, cluster_id, member_order):
    mine = (embeddings, cluster_id, member_order)
    width = embeddings.shape[1]
    hold = lax.optimization_barrier
    own = own_call(prepare_kernel, jax.ShapeDtypeStruct((AUG, width), jnp.bfloat16), *mine)
    cols = lax.all_gather(own, ("z", "core"), axis=0, tiled=True)

    up = lambda v: lax.ppermute(v, "y", ring(8, 1))
    down = lambda v: lax.ppermute(v, "y", ring(8, -1))
    u1, d1 = up(own), down(own)
    known = own_call(remember_kernel, jax.ShapeDtypeStruct((2, ROWS), jnp.float32), *mine)
    u1, known = hold((u1, known))
    u2, d2 = up(u1), down(d1)
    u3, d3 = up(u2), down(d2)
    u4 = up(u3)
    place = lax.axis_index("y").astype(jnp.int32).reshape(1)
    slots, slot_meta = spread(place, [own, u1, d1, u2, d2, u3, d3], (0, 7, 1, 6, 2, 5, 3))

    found = match(place, u4, 4, slots, slot_meta, cols).reshape(CLUSTERS, 8, SLOTS)
    found = found.transpose(1, 0, 2).reshape(8, 1, CLUSTERS * SLOTS)
    arrived = lax.all_to_all(found, "y", split_axis=0, concat_axis=0, tiled=True)
    return collect(arrived, known)[0]


def solution(mesh):
    axes = ("x", "z", "core", "y")
    finer = Mesh(mesh.devices.reshape(mesh.shape["outer"], 8, 2, 8), axes)
    return jax.shard_map(
        per_device,
        mesh=finer,
        in_specs=(P(axes, None), P(axes), P(axes)),
        out_specs=P(axes),
        check_vma=False,
    )
```
